32 devices in a mesh: dp: 8 (over z, y), mp: 4 (over x, core).
Axes of the slice: x: 2, y: 2, z: 4, core: 2. Of those that a mesh axis runs over, the one named last changes fastest.
Arguments:
- tokens: bfloat16 [1536, 1152], P('dp'), may hold values from -6 to 6
- doc_lengths: int32 [16, 2], P('dp'), may hold values from 1 to 48, as said below
- cotangent: bfloat16 [1536, 1152], P('dp'), may hold values from -6 to 6
- query_weight: bfloat16 [1152, 1024], P('dp', 'mp'), may hold values from -0.1875 to 0.1875
- key_weight: bfloat16 [1152, 256], P('dp'), may hold values from -0.1875 to 0.1875
- value_weight: bfloat16 [1152, 256], P('dp'), may hold values from -0.1875 to 0.1875
- out_weight: bfloat16 [1024, 1152], P('mp', 'dp'), may hold values from -0.1875 to 0.1875
- gate_weight: bfloat16 [1152, 6912], P('dp', 'mp'), may hold values from -0.1875 to 0.1875
- up_weight: bfloat16 [1152, 6912], P('dp', 'mp'), may hold values from -0.1875 to 0.1875
- down_weight: bfloat16 [6912, 1152], P('mp', 'dp'), may hold values from -0.078125 to 0.078125
- pre_attn_gain: bfloat16 [1152], P('dp'), may hold values from 0.5 to 1.5
- post_attn_gain: bfloat16 [1152], P('dp'), may hold values from 0.5 to 1.5
- pre_ffn_gain: bfloat16 [1152], P('dp'), may hold values from 0.5 to 1.5
- post_ffn_gain: bfloat16 [1152], P('dp'), may hold values from 0.5 to 1.5
- query_gain: bfloat16 [256], P('dp'), may hold values from 0.5 to 1.5
- key_gain: bfloat16 [256], P('dp'), may hold values from 0.5 to 1.5
Outputs:
- mixed: bfloat16 [1536, 1152], P('dp')
- tokens_grad: float32 [1536, 1152], P('dp')
- query_grad: float32 [1152, 1024], P('dp', 'mp')
- key_grad: float32 [1152, 256], P('dp')
- value_grad: float32 [1152, 256], P('dp')
- out_grad: float32 [1024, 1152], P('mp', 'dp')
- gate_grad: float32 [1152, 6912], P('dp', 'mp')
- up_grad: float32 [1152, 6912], P('dp', 'mp')
- down_grad: float32 [6912, 1152], P('mp', 'dp')
- pre_attn_grad: float32 [1152], P('dp')
- post_attn_grad: float32 [1152], P('dp')
- pre_ffn_grad: float32 [1152], P('dp')
- post_ffn_grad: float32 [1152], P('dp')
- query_gain_grad: float32 [256], P('dp')
- key_gain_grad: float32 [256], P('dp')
The draws below stay inside these ranges and needn't reach their ends.
Inputs may be any that keep to these rules, and one draw needn't show every extreme that they name: Row b of doc_lengths gives the 2 document lengths of buffer b, the buffers of one index of dp being 2 consecutive rows; the documents lie end to end from the buffer's first row, and the rows after them are padding.
All inputs are finite; a program needn't handle non-finite values.
Results may differ from the reference program's by a relative error of at most 0.019.
Values may be sent and summed in bfloat16 or wider, within the bound.
A program may use at most 128 MiB of HBM per device.

```python
import jax
import jax.numpy as jnp
from jax import lax

D = 1152
NQ = 4
HD = 256
FF = 6912
WINDOW = 512
DOCS = 2
ROWS = 96
MOST = 48
BUFFERS = 16
TOKENS = 1536


def draw_doc_lengths(key, part):
    drawn = jax.random.randint(jax.random.fold_in(key, 11), (BUFFERS, DOCS), 1, MOST + 1)
    chosen_row = jax.random.randint(jax.random.fold_in(key, 12), (), 0, BUFFERS)
    chosen_col = jax.random.randint(jax.random.fold_in(key, 13), (), 0, DOCS)
    row_index = jnp.arange(BUFFERS)[:, None]
    col_index = jnp.arange(DOCS)[None, :]
    chosen = (row_index == chosen_row) & (col_index == chosen_col)
    return jnp.where(chosen, MOST, drawn).astype(jnp.int32)


def shard_levels(stream_key, extent, split, low, largest):
    gain, own = 1.0, jax.random.fold_in(stream_key, 6)
    for dim, shards_of in split:
        heights = jnp.exp(jax.random.uniform(jax.random.fold_in(own, dim), (shards_of,), jnp.float32, low / len(split), largest / len(split)))
        gain = gain * jnp.repeat(heights, extent[dim] // shards_of).reshape([-1 if axis == dim else 1 for axis in range(len(extent))])
    return gain


def centred(key, shape, deviation, limit, pieces=(), kind=jnp.bfloat16):
    level = shard_levels(key, shape, pieces, -0.22, 0.18) if pieces else 1.0
    array = jax.random.normal(key, shape, jnp.float32) * deviation * level
    return jnp.minimum(jnp.maximum(array, -limit), limit).astype(kind)


def setup_inputs(seed: int = 0) -> dict:
    arg_keys = jax.random.split(jax.random.key(seed), 17)
    return {
        "tokens": centred(arg_keys[0], (TOKENS, D), 1.0, 6.0, ((0, 8),)),
        "doc_lengths": draw_doc_lengths(jax.random.fold_in(arg_keys[16], 71), 0),
        "cotangent": centred(arg_keys[2], (TOKENS, D), 1.0, 6.0, ((0, 8),)),
        "query_weight": centred(arg_keys[3], (D, NQ * HD), D ** -0.5, 0.1875, ((0, 8), (1, 4))),
        "key_weight": centred(arg_keys[4], (D, HD), D ** -0.5, 0.1875, ((0, 8),)),
        "value_weight": centred(arg_keys[5], (D, HD), D ** -0.5, 0.1875, ((0, 8),)),
        "out_weight": centred(arg_keys[6], (NQ * HD, D), (NQ * HD) ** -0.5, 0.1875, ((0, 4), (1, 8))),
        "gate_weight": centred(arg_keys[7], (D, FF), D ** -0.5, 0.1875, ((0, 8), (1, 4))),
        "up_weight": centred(arg_keys[8], (D, FF), D ** -0.5, 0.1875, ((0, 8), (1, 4))),
        "down_weight": centred(arg_keys[9], (FF, D), FF ** -0.5, 0.078125, ((0, 4), (1, 8))),
        "pre_attn_gain": jnp.clip(1.0 + 0.1 * jax.random.normal(arg_keys[10], (D,), jnp.float32), 0.5, 1.5).astype(jnp.bfloat16),
        "post_attn_gain": jnp.clip(1.0 + 0.1 * jax.random.normal(arg_keys[11], (D,), jnp.float32), 0.5, 1.5).astype(jnp.bfloat16),
        "pre_ffn_gain": jnp.clip(1.0 + 0.1 * jax.random.normal(arg_keys[12], (D,), jnp.float32), 0.5, 1.5).astype(jnp.bfloat16),
        "post_ffn_gain": jnp.clip(1.0 + 0.1 * jax.random.normal(arg_keys[13], (D,), jnp.float32), 0.5, 1.5).astype(jnp.bfloat16),
        "query_gain": jnp.clip(1.0 + 0.1 * jax.random.normal(arg_keys[14], (HD,), jnp.float32), 0.5, 1.5).astype(jnp.bfloat16),
        "key_gain": jnp.clip(1.0 + 0.1 * jax.random.normal(arg_keys[15], (HD,), jnp.float32), 0.5, 1.5).astype(jnp.bfloat16),
    }


@jax.custom_vjp
def low(v):
    return lax.optimization_barrier(v.astype(jnp.bfloat16)).astype(jnp.float32)

@jax.custom_vjp
def low_back(v):
    return v

def low_keep(v):
    return (low(v), None)

def low_pass(kept, grad):
    return (grad,)

def back_keep(v):
    return (v, None)

def back_low(kept, grad):
    return (low(grad),)
low.defvjp(low_keep, low_pass)
low_back.defvjp(back_keep, back_low)
EPSILON = 1e-06
THETA_BASE = 10000.0
NEGATIVE = -1e+30
HIGHEST = lax.Precision.HIGHEST

def product(left_op, right_op):
    return jnp.dot(left_op, right_op, precision=HIGHEST)

def normed(values, factor):
    return values * lax.rsqrt(lax.optimization_barrier(jnp.mean(values * values, axis=-1, keepdims=True)) + EPSILON) * factor

def rotate(values, cosine, sine_table):
    half_width = values.shape[-1] // 2
    leading = values[..., :half_width]
    trailing = values[..., half_width:]
    return jnp.concatenate([leading * cosine - trailing * sine_table, trailing * cosine + leading * sine_table], axis=-1)

def layout(lengths, row_count):
    doc_ends = jnp.cumsum(lengths).astype(jnp.int32)
    row_index = jnp.arange(row_count, dtype=jnp.int32)
    passed = row_index[:, None] >= doc_ends[None, :]
    segment = lax.optimization_barrier(jnp.sum(passed.astype(jnp.int32), axis=1)).astype(jnp.int32)
    begins = lax.optimization_barrier(jnp.sum(jnp.where(passed, lengths[None, :], 0), axis=1)).astype(jnp.int32)
    position = row_index - begins
    live_rows = (segment < lengths.shape[0]).astype(jnp.float32)
    allowed = (segment[:, None] == segment[None, :]) & (row_index[None, :] <= row_index[:, None]) & (row_index[:, None] - row_index[None, :] < WINDOW)
    return (position, live_rows, allowed)

def angles(position, head_width):
    half_width = head_width // 2
    frequency = THETA_BASE ** (-2.0 * jnp.arange(half_width, dtype=jnp.float32) / head_width)
    turned = position.astype(jnp.float32)[:, None] * frequency[None, :]
    return (jnp.cos(turned), jnp.sin(turned))

def block(inputs, lengths, params):
    query_w, key_w, value_w, out_w, gate_w, up_w, down_w, gain_one, gain_two, gain_three, gain_four, query_g, key_g = params
    row_count = inputs.shape[0]
    position, live_rows, allowed = layout(lengths, row_count)
    cosine, sine_table = angles(position, HD)
    cosine = cosine[:, None, :]
    sine_table = sine_table[:, None, :]
    normed_in = low(normed(inputs, gain_one))
    query_pre = low_back(product(normed_in, query_w).reshape(row_count, NQ, HD))
    key_pre = low_back(jnp.broadcast_to(product(normed_in, key_w)[:, None, :], (row_count, NQ, HD)))
    value_rows = low_back(jnp.broadcast_to(low(product(normed_in, value_w))[:, None, :], (row_count, NQ, HD)))
    query_rot = low(rotate(normed(query_pre, query_g), cosine, sine_table))
    key_rot = low(rotate(normed(key_pre, key_g), cosine, sine_table))
    scores = low_back(jnp.einsum('qhd,khd->hqk', query_rot, key_rot, precision=HIGHEST) * HD ** (-0.5))
    scores = jnp.where(allowed[None], scores, NEGATIVE)
    row_peak = lax.optimization_barrier(jnp.max(scores, axis=-1, keepdims=True))
    raised = jnp.exp(scores - row_peak)
    attention = low(raised / lax.optimization_barrier(jnp.sum(raised, axis=-1, keepdims=True)))
    attended = low_back(low(jnp.einsum('hqk,khd->qhd', attention, value_rows, precision=HIGHEST))).reshape(row_count, NQ * HD)
    attn_sum = low_back(product(attended, out_w))
    middle = inputs + normed(attn_sum, gain_two) * live_rows[:, None]
    normed_mid = low(normed(middle, gain_three))
    gate_proj = low_back(product(normed_mid, gate_w))
    up_proj = low_back(product(normed_mid, up_w))
    hidden = low(jax.nn.gelu(gate_proj, approximate=True) * up_proj)
    ffn_sum = low_back(product(hidden, down_w))
    return middle + normed(ffn_sum, gain_four) * live_rows[:, None]

def reference(tokens, doc_lengths, cotangent, query_weight, key_weight, value_weight, out_weight, gate_weight, up_weight, down_weight, pre_attn_gain, post_attn_gain, pre_ffn_gain, post_ffn_gain, query_gain, key_gain):
    params = tuple((member.astype(jnp.float32) for member in (query_weight, key_weight, value_weight, out_weight, gate_weight, up_weight, down_weight, pre_attn_gain, post_attn_gain, pre_ffn_gain, post_ffn_gain, query_gain, key_gain)))
    inputs_all = tokens.astype(jnp.float32).reshape(BUFFERS, ROWS, D)
    upstream_all = cotangent.astype(jnp.float32).reshape(BUFFERS, ROWS, D)

    def forward(inputs_whole, weights_whole):

        def one_buffer(buffer_args):
            return block(buffer_args[0], buffer_args[1], weights_whole)
        return lax.map(jax.checkpoint(one_buffer), (inputs_whole, doc_lengths))
    output_all, backward = jax.vjp(forward, inputs_all, params)
    d_inputs, d_params = backward(upstream_all)
    return (output_all.reshape(TOKENS, D).astype(jnp.bfloat16), d_inputs.reshape(TOKENS, D), d_params[0], d_params[1], d_params[2], d_params[3], d_params[4], d_params[5], d_params[6], d_params[7], d_params[8], d_params[9], d_params[10], d_params[11], d_params[12])
```

```python
import jax
import jax.numpy as jnp
from jax import lax
from jax.sharding import PartitionSpec as P

WINDOW = 512


EPSILON = 1e-06
THETA_BASE = 10000.0
NEGATIVE = -1e30


def matmul(left_op, right_op):
    return jnp.dot(left_op, right_op, preferred_element_type=jnp.float32)


def inner_rows(left_op, right_op):
    return lax.dot_general(
        left_op, right_op, (((0,), (0,)), ((), ())), preferred_element_type=jnp.float32
    )


def inner_cols(left_op, right_op):
    return lax.dot_general(
        left_op, right_op, (((1,), (1,)), ((), ())), preferred_element_type=jnp.float32
    )


def normed(values, factor):
    return values * lax.rsqrt(jnp.mean(values * values, axis=-1, keepdims=True) + EPSILON) * factor


def rotate(values, cosine, sine_table):
    half_width = values.shape[-1] // 2
    leading = values[..., :half_width]
    trailing = values[..., half_width:]
    return jnp.concatenate(
        [leading * cosine - trailing * sine_table, trailing * cosine + leading * sine_table],
        axis=-1,
    )


def layout(lengths, row_count):
    batches, docs = lengths.shape
    total = batches * row_count
    index = jnp.arange(total, dtype=jnp.int32)
    buffer = index // row_count
    inside = index % row_count
    order = jnp.arange(docs, dtype=jnp.int32)
    ends = jnp.sum(
        jnp.where(order[None, :, None] >= order[None, None, :], lengths[:, None, :], 0), axis=2
    )
    row_ends = jnp.repeat(ends, row_count, axis=0)
    row_lengths = jnp.repeat(lengths, row_count, axis=0)
    passed = inside[:, None] >= row_ends
    segment = jnp.sum(passed.astype(jnp.int32), axis=1)
    begins = jnp.sum(jnp.where(passed, row_lengths, 0), axis=1)
    position = inside - begins
    live_rows = (segment < docs).astype(jnp.float32)
    group = buffer * (docs + 1) + segment
    allowed = (
        (group[:, None] == group[None, :])
        & (index[None, :] <= index[:, None])
        & (index[:, None] - index[None, :] < WINDOW)
    )
    return (position, live_rows, allowed)


def angles(position, head_width):
    half_width = head_width // 2
    frequency = THETA_BASE ** (-2.0 * jnp.arange(half_width, dtype=jnp.float32) / head_width)
    turned = position.astype(jnp.float32)[:, None] * frequency[None, :]
    return (jnp.cos(turned), jnp.sin(turned))


def on_device(
    tokens,
    doc_lengths,
    cotangent,
    query_weight,
    key_weight,
    value_weight,
    out_weight,
    gate_weight,
    up_weight,
    down_weight,
    pre_attn_gain,
    post_attn_gain,
    pre_ffn_gain,
    post_ffn_gain,
    query_gain,
    key_gain,
):
    low = jnp.bfloat16
    full = jnp.float32
    dp = lax.axis_size("dp")
    mp = lax.axis_size("mp")
    shard = lax.axis_index("mp")
    rows, width = tokens.shape
    share = width // dp
    head_width = query_weight.shape[1]
    units = gate_weight.shape[1] // dp
    own_rows = rows // mp
    own = (shard * own_rows, own_rows)

    gain_head = query_gain.shape[0]
    gains = jnp.concatenate(
        [pre_attn_gain, post_attn_gain, pre_ffn_gain, post_ffn_gain, query_gain, key_gain]
    )
    block = jnp.concatenate([query_weight, key_weight, value_weight, out_weight.T], axis=1)
    gains_row = jnp.pad(gains, (0, block.shape[1] - gains.shape[0]))[None]
    packed = jnp.concatenate([block, jnp.pad(gains_row, ((0, 15), (0, 0)))], axis=0)
    packed = lax.all_gather(packed, "dp", axis=0, tiled=False)
    attn_w = packed[:, :share].reshape(width, 4 * head_width)
    qkv_w = attn_w[:, : 3 * head_width]
    out_wt = attn_w[:, 3 * head_width :]
    all_gains = packed[:, share].astype(full)
    gain_one, gain_two, gain_three, gain_four = (
        all_gains[:, i * share : (i + 1) * share].reshape(width) for i in range(4)
    )
    query_g = all_gains[:, 4 * share : 4 * share + gain_head].reshape(head_width)
    key_g = all_gains[:, 4 * share + gain_head : 4 * share + 2 * gain_head].reshape(head_width)

    ffn_block = jnp.stack([gate_weight, up_weight, down_weight.T], axis=0)
    ffn_block = ffn_block.reshape(3, share, dp, units).transpose(2, 1, 0, 3)
    ffn_block = ffn_block.reshape(dp, share, 3 * units)
    ffn_w = lax.all_to_all(ffn_block, "dp", split_axis=0, concat_axis=0, tiled=True)
    ffn_w = ffn_w.reshape(width, 3 * units)
    glu_w = ffn_w[:, : 2 * units]
    down_wt = ffn_w[:, 2 * units :]

    inputs = tokens.astype(full)
    position, live_rows, allowed = layout(doc_lengths, rows // doc_lengths.shape[0])
    cosine, sine_table = angles(position, head_width)
    normed_in = normed(inputs, gain_one).astype(low)
    projected = matmul(normed_in, qkv_w)
    query_pre = projected[:, :head_width]
    key_pre = projected[:, head_width : 2 * head_width]
    value_low = projected[:, 2 * head_width :].astype(low)
    query_low = rotate(normed(query_pre, query_g), cosine, sine_table).astype(low)
    key_low = rotate(normed(key_pre, key_g), cosine, sine_table).astype(low)
    score_scale = head_width ** (-0.5)
    scores = inner_cols(query_low, key_low) * score_scale
    scores = jnp.where(allowed, scores, NEGATIVE)
    row_peak = jnp.max(scores, axis=1, keepdims=True)
    raised = jnp.exp(scores - row_peak)
    attention = raised / jnp.sum(raised, axis=1, keepdims=True)
    attention_low = attention.astype(low)
    attended = matmul(attention_low, value_low).astype(low)
    attn_part = inner_cols(attended, out_wt).astype(low)
    attn_sum = lax.psum_scatter(attn_part, "mp", scatter_dimension=0, tiled=True).astype(full)

    inputs_own = lax.dynamic_slice_in_dim(tokens, *own, axis=0).astype(full)
    upstream = lax.dynamic_slice_in_dim(cotangent, *own, axis=0).astype(full)
    live = lax.dynamic_slice_in_dim(live_rows, *own, axis=0)[:, None]

    def post_norm(values, factor):
        return normed(values, factor) * live

    attn_out, back_two = jax.vjp(post_norm, attn_sum, gain_two)
    middle = inputs_own + attn_out
    normed_mid_own, back_three = jax.vjp(normed, middle, gain_three)
    normed_mid = lax.all_gather(normed_mid_own.astype(low), ("dp", "mp"), axis=0, tiled=True)
    glu_pre = matmul(normed_mid, glu_w)
    gate_proj = glu_pre[:, :units]
    up_proj = glu_pre[:, units:]

    def glu(gate_in, up_in):
        return jax.nn.gelu(gate_in, approximate=True) * up_in

    hidden_full, back_glu = jax.vjp(glu, gate_proj, up_proj)
    hidden = hidden_full.astype(low)
    ffn_part = inner_cols(hidden, down_wt).astype(low)
    ffn_sum = lax.psum_scatter(ffn_part, ("dp", "mp"), scatter_dimension=0, tiled=True).astype(full)
    ffn_out, back_four = jax.vjp(post_norm, ffn_sum, gain_four)
    mixed_own = (middle + ffn_out).astype(low)

    d_ffn_own, grad_four = back_four(upstream)
    d_ffn = lax.all_gather(d_ffn_own.astype(low), ("dp", "mp"), axis=0, tiled=True)
    grad_down_t = inner_rows(d_ffn, hidden)
    d_hidden = matmul(d_ffn, down_wt)
    d_gate, d_up = back_glu(d_hidden)
    d_glu = jnp.concatenate([d_gate.astype(low), d_up.astype(low)], axis=1)
    d_mid_part = inner_cols(d_glu, glu_w).astype(low)
    d_mid = lax.psum_scatter(d_mid_part, ("dp", "mp"), scatter_dimension=0, tiled=True).astype(full)
    grad_glu = inner_rows(normed_mid, d_glu)
    ffn_grad = jnp.concatenate([grad_glu, grad_down_t], axis=1).astype(low)
    ffn_grad = ffn_grad.reshape(dp, share, 3 * units)
    ffn_grad = lax.all_to_all(ffn_grad, "dp", split_axis=0, concat_axis=0, tiled=True)
    ffn_grad = ffn_grad.reshape(dp, share, 3, units).transpose(2, 1, 0, 3)
    ffn_grad = ffn_grad.reshape(3, share, dp * units).astype(full)

    d_mid_add, grad_three = back_three(d_mid)
    d_middle = upstream + d_mid_add
    d_attn_own, grad_two = back_two(d_middle)
    d_attn = lax.all_gather(d_attn_own.astype(low), "mp", axis=0, tiled=True)

    grad_out_t = inner_rows(d_attn, attended)
    d_attended = matmul(d_attn, out_wt).astype(low)
    d_value = inner_rows(attention_low, d_attended).astype(low)
    d_probs = inner_cols(d_attended, value_low)
    d_scores = attention * (d_probs - jnp.sum(attention * d_probs, axis=1, keepdims=True))
    d_scores = d_scores.astype(low)
    d_query_rot = matmul(d_scores, key_low) * score_scale
    d_key_rot = inner_rows(d_scores, query_low) * score_scale

    def turned(values, factor):
        return rotate(normed(values, factor), cosine, sine_table)

    _, back_query = jax.vjp(turned, query_pre, query_g)
    d_query_pre, grad_qgain = back_query(d_query_rot)
    _, back_key = jax.vjp(turned, key_pre, key_g)
    d_key_pre, grad_kgain = back_key(d_key_rot)
    d_qkv = jnp.concatenate([d_query_pre.astype(low), d_key_pre.astype(low), d_value], axis=1)
    d_in_part = inner_cols(d_qkv, qkv_w).astype(low)
    d_in = lax.psum_scatter(d_in_part, "mp", scatter_dimension=0, tiled=True).astype(full)
    grad_qkv = inner_rows(normed_in, d_qkv)
    _, back_one = jax.vjp(normed, inputs_own, gain_one)
    d_in_add, grad_one = back_one(d_in)
    tokens_grad_own = d_middle + d_in_add

    pieces = [g.reshape(dp, -1) for g in (grad_one, grad_two, grad_three, grad_four, grad_qgain, grad_kgain)]
    gains_grad = jnp.concatenate(pieces, axis=1)
    gains_grad = jnp.pad(gains_grad, ((0, 0), (0, 4 * head_width - gains_grad.shape[1])))
    weights_grad = jnp.concatenate([grad_qkv, grad_out_t], axis=1).reshape(dp, share, 4 * head_width)
    owned = jnp.concatenate(
        [weights_grad, jnp.pad(gains_grad[:, None], ((0, 0), (0, 15), (0, 0)))], axis=1
    ).astype(low)
    owned = lax.psum_scatter(owned, "dp", scatter_dimension=0, tiled=True)[0].astype(full)
    shared = jnp.concatenate(
        [
            owned[:share, head_width : 3 * head_width].reshape(-1),
            owned[share, : 4 * share + 2 * gain_head],
        ]
    )
    shared = lax.psum(shared, "mp")
    kv_grad = shared[: 2 * share * head_width].reshape(share, 2 * head_width)
    gain_out = shared[2 * share * head_width :]
    mixed = lax.all_gather(mixed_own, "mp", axis=0, tiled=True)
    tokens_grad = lax.all_gather(tokens_grad_own.astype(low), "mp", axis=0, tiled=True).astype(full)
    return (
        mixed,
        tokens_grad,
        owned[:share, :head_width],
        kv_grad[:, :head_width],
        kv_grad[:, head_width:],
        owned[:share, 3 * head_width :].T,
        ffn_grad[0],
        ffn_grad[1],
        ffn_grad[2].T,
        gain_out[:share],
        gain_out[share : 2 * share],
        gain_out[2 * share : 3 * share],
        gain_out[3 * share : 4 * share],
        gain_out[4 * share : 4 * share + gain_head],
        gain_out[4 * share + gain_head :],
    )


def solution(mesh):
    placed = (
        P("dp", None),
        P("dp", None),
        P("dp", None),
        P("dp", "mp"),
        P("dp", None),
        P("dp", None),
        P("mp", "dp"),
        P("dp", "mp"),
        P("dp", "mp"),
        P("mp", "dp"),
        P("dp"),
        P("dp"),
        P("dp"),
        P("dp"),
        P("dp"),
        P("dp"),
    )
    return jax.shard_map(
        on_device,
        mesh=mesh,
        in_specs=placed,
        out_specs=(
            P("dp", None),
            P("dp", None),
            P("dp", "mp"),
            P("dp", None),
            P("dp", None),
            P("mp", "dp"),
            P("dp", "mp"),
            P("dp", "mp"),
            P("mp", "dp"),
            P("dp"),
            P("dp"),
            P("dp"),
            P("dp"),
            P("dp"),
            P("dp"),
        ),
        check_vma=False,
    )
```

```python
import functools
import math

import jax
import jax.numpy as jnp
from jax import lax
from jax.experimental import pallas as pl
from jax.experimental.pallas import tpu as pltpu
from jax.sharding import PartitionSpec as P

WINDOW = 512


EPSILON = 1e-06
THETA_BASE = 10000.0
NEGATIVE = -1e30


def matmul(left_op, right_op):
    return jnp.dot(left_op, right_op, preferred_element_type=jnp.float32)


def inner_rows(left_op, right_op):
    return lax.dot_general(
        left_op, right_op, (((0,), (0,)), ((), ())), preferred_element_type=jnp.float32
    )


def inner_cols(left_op, right_op):
    return lax.dot_general(
        left_op, right_op, (((1,), (1,)), ((), ())), preferred_element_type=jnp.float32
    )


def normed(values, factor):
    return values * lax.rsqrt(jnp.mean(values * values, axis=-1, keepdims=True) + EPSILON) * factor


def rotate(values, cosine, sine_table):
    half_width = values.shape[-1] // 2
    leading = values[..., :half_width]
    trailing = values[..., half_width:]
    return jnp.concatenate(
        [leading * cosine - trailing * sine_table, trailing * cosine + leading * sine_table],
        axis=-1,
    )


def layout(lengths, row_count):
    batches, docs = lengths.shape
    total = batches * row_count
    index = jnp.arange(total, dtype=jnp.int32)
    buffer = index // row_count
    inside = index % row_count
    order = jnp.arange(docs, dtype=jnp.int32)
    ends = jnp.sum(
        jnp.where(order[None, :, None] >= order[None, None, :], lengths[:, None, :], 0), axis=2
    )
    row_ends = jnp.repeat(ends, row_count, axis=0)
    row_lengths = jnp.repeat(lengths, row_count, axis=0)
    passed = inside[:, None] >= row_ends
    segment = jnp.sum(passed.astype(jnp.int32), axis=1)
    begins = jnp.sum(jnp.where(passed, row_lengths, 0), axis=1)
    position = inside - begins
    live_rows = (segment < docs).astype(jnp.float32)
    group = buffer * (docs + 1) + segment
    allowed = (
        (group[:, None] == group[None, :])
        & (index[None, :] <= index[:, None])
        & (index[:, None] - index[None, :] < WINDOW)
    )
    return (position, live_rows, allowed)


def angles(position, head_width):
    half_width = head_width // 2
    frequency = THETA_BASE ** (-2.0 * jnp.arange(half_width, dtype=jnp.float32) / head_width)
    turned = position.astype(jnp.float32)[:, None] * frequency[None, :]
    return (jnp.cos(turned), jnp.sin(turned))


MESH = pl.DeviceIdType.MESH


def axis_factors(axes):
    dims = []
    for axis in axes:
        left = lax.axis_size(axis)
        while left > 1:
            size = 4 if axis == "dp" and left >= 8 else 2
            left //= size
            dims.append((axis, size, left))
    return dims


def chunk_orders(dims, width):
    order = list(reversed(range(len(dims))))
    lanes = width // 128
    if dims[0][0] != "dp" or width % 128 or lanes < 2:
        return [(0, width, order)]
    swapped = list(order)
    at = 1 if len(dims) >= 3 else 0
    swapped[at], swapped[at + 1] = swapped[at + 1], swapped[at]
    half = (lanes + 1) // 2 * 128
    return [(0, half, order), (half, width - half, swapped)]


def places(dims):
    return [lax.rem(lax.axis_index(axis) // stride, size) for axis, size, stride in dims]


def peer(dims, coords, which, step):
    axis, size, stride = dims[which]
    target = lax.rem(coords[which] + step, size)
    device = {name: lax.axis_index(name) for name in ("dp", "mp")}
    device[axis] = device[axis] + (target - coords[which]) * stride
    return target, (device["dp"], device["mp"])


def greet(dims, coords):
    barrier = pltpu.get_barrier_semaphore()
    count = 0
    for which, (_, size, _) in enumerate(dims):
        for step in range(1, size):
            _, device = peer(dims, coords, which, step)
            pl.semaphore_signal(barrier, inc=1, device_id=device, device_id_type=MESH)
            count += 1
    pl.semaphore_wait(barrier, count)


def slots_of(dims):
    firsts, total = [], 0
    for _, size, _ in dims:
        firsts.append(total)
        total += size - 1
    return firsts, total


def gather_kernel(dims, chunks, firsts, x_ref, o_ref, send_sem, recv_sem):
    coords = places(dims)
    o_ref[tuple(coords)] = x_ref[...]
    greet(dims, coords)

    def begin(k, stage):
        first, columns, order = chunks[k]
        order = order[::-1]
        done = order[:stage]
        which = order[stage]
        index = tuple(
            pl.ds(0, dims[i][1]) if i in done else coords[i] for i in range(len(dims))
        )
        block = o_ref.at[index + (slice(None), pl.ds(first, columns))]
        copies = []
        for step in range(1, dims[which][1]):
            slot = firsts[which] + step - 1
            _, device = peer(dims, coords, which, step)
            copy = pltpu.make_async_remote_copy(
                src_ref=block,
                dst_ref=block,
                send_sem=send_sem.at[k, slot],
                recv_sem=recv_sem.at[k, slot],
                device_id=device,
                device_id_type=MESH,
            )
            copy.start()
            copies.append(copy)
        return copies

    flying = [begin(k, 0) for k in range(len(chunks))]
    for stage in range(len(dims)):
        for k in range(len(chunks)):
            for copy in flying[k]:
                copy.wait()
            if stage + 1 < len(dims):
                flying[k] = begin(k, stage + 1)


def gather(x, axes, ident):
    dims = axis_factors(axes)
    rows, width = x.shape
    chunks = chunk_orders(dims, width)
    firsts, slots = slots_of(dims)
    sizes = tuple(size for _, size, _ in dims)
    count = math.prod(sizes)
    nbytes = count * rows * width * x.dtype.itemsize
    out = pl.pallas_call(
        functools.partial(gather_kernel, dims, chunks, firsts),
        out_shape=jax.ShapeDtypeStruct(sizes + (rows, width), x.dtype),
        in_specs=[pl.BlockSpec(memory_space=pltpu.VMEM)],
        out_specs=pl.BlockSpec(memory_space=pltpu.VMEM),
        scratch_shapes=[
            pltpu.SemaphoreType.DMA((len(chunks), slots)),
            pltpu.SemaphoreType.DMA((len(chunks), slots)),
        ],
        compiler_params=pltpu.CompilerParams(
            collective_id=ident, has_side_effects=True, vmem_limit_bytes=nbytes + (8 << 20)
        ),
        cost_estimate=pl.CostEstimate(flops=0, bytes_accessed=20 * nbytes, transcendentals=0),
    )(x)
    return out.reshape(count, rows, width)


def scatter_kernel(dims, chunks, firsts, x_ref, o_ref, acc, send_sem, recv_sem, *landed):
    coords = places(dims)
    greet(dims, coords)
    total = len(dims)

    def begin(k, stage):
        first, columns, order = chunks[k]
        done = order[:stage]
        which = order[stage]
        source = x_ref if stage == 0 else acc
        copies = []
        for step in range(1, dims[which][1]):
            slot = firsts[which] + step - 1
            target, device = peer(dims, coords, which, step)
            index = tuple(
                target if i == which else coords[i] if i in done else pl.ds(0, dims[i][1])
                for i in range(total)
            )
            copy = pltpu.make_async_remote_copy(
                src_ref=source.at[index + (slice(None), pl.ds(first, columns))],
                dst_ref=landed[k * total + stage].at[step - 1],
                send_sem=send_sem.at[k, slot],
                recv_sem=recv_sem.at[k, slot],
                device_id=device,
                device_id_type=MESH,
            )
            copy.start()
            copies.append(copy)
        return copies

    def add(k, stage):
        first, columns, order = chunks[k]
        which = order[stage]
        remain = [i for i in range(total) if i not in order[: stage + 1]]
        source = x_ref if stage == 0 else acc
        got = landed[k * total + stage]
        count = math.prod(dims[i][1] for i in remain)

        def one(n, carry):
            inner, left = {}, n
            for i in reversed(remain):
                inner[i] = lax.rem(left, dims[i][1])
                left = left // dims[i][1]
            index = tuple(inner[i] if i in inner else coords[i] for i in range(total))
            own = source[index + (slice(None), pl.ds(first, columns))].astype(jnp.float32)
            for step in range(1, dims[which][1]):
                place = (step - 1,) + tuple(inner[i] for i in remain)
                own = own + got[place].astype(jnp.float32)
            if remain:
                acc[index + (slice(None), pl.ds(first, columns))] = own.astype(acc.dtype)
            else:
                o_ref[:, pl.ds(first, columns)] = own
            return carry

        if count == 1:
            one(0, 0)
        else:
            lax.fori_loop(0, count, one, 0)

    flying = [begin(k, 0) for k in range(len(chunks))]
    for stage in range(total):
        for k in range(len(chunks)):
            for copy in flying[k]:
                copy.wait()
            add(k, stage)
            if stage + 1 < total:
                flying[k] = begin(k, stage + 1)


def scatter(x, axes, ident):
    dims = axis_factors(axes)
    _, rows, width = x.shape
    chunks = chunk_orders(dims, width)
    firsts, slots = slots_of(dims)
    sizes = tuple(size for _, size, _ in dims)
    landed = []
    for _, columns, order in chunks:
        for stage, which in enumerate(order):
            remain = tuple(sizes[i] for i in range(len(dims)) if i not in order[: stage + 1])
            landed.append(
                pltpu.VMEM((sizes[which] - 1,) + remain + (rows, columns), x.dtype)
            )
    nbytes = math.prod(sizes) * rows * width * x.dtype.itemsize
    return pl.pallas_call(
        functools.partial(scatter_kernel, dims, chunks, firsts),
        out_shape=jax.ShapeDtypeStruct((rows, width), jnp.float32),
        in_specs=[pl.BlockSpec(memory_space=pltpu.VMEM)],
        out_specs=pl.BlockSpec(memory_space=pltpu.VMEM),
        scratch_shapes=[
            pltpu.VMEM(sizes + (rows, width), x.dtype),
            pltpu.SemaphoreType.DMA((len(chunks), slots)),
            pltpu.SemaphoreType.DMA((len(chunks), slots)),
            *landed,
        ],
        compiler_params=pltpu.CompilerParams(
            collective_id=ident, has_side_effects=True, vmem_limit_bytes=3 * nbytes + (8 << 20)
        ),
        cost_estimate=pl.CostEstimate(flops=0, bytes_accessed=20 * nbytes, transcendentals=0),
    )(x.reshape(sizes + (rows, width)))


def exchange_kernel(parts, x_ref, o_ref, local_sem, send_sem, recv_sem):
    me = lax.axis_index("dp")
    other = lax.axis_index("mp")
    barrier = pltpu.get_barrier_semaphore()
    for step in range(1, parts):
        device = (lax.rem(me + step, parts), other)
        pl.semaphore_signal(barrier, inc=1, device_id=device, device_id_type=MESH)
    pl.semaphore_wait(barrier, parts - 1)
    copies = []
    for step in range(1, parts):
        target = lax.rem(me + step, parts)
        copy = pltpu.make_async_remote_copy(
            src_ref=x_ref.at[target],
            dst_ref=o_ref.at[me],
            send_sem=send_sem.at[step - 1],
            recv_sem=recv_sem.at[step - 1],
            device_id=(target, other),
            device_id_type=MESH,
        )
        copy.start()
        copies.append(copy)
    own = pltpu.make_async_copy(x_ref.at[me], o_ref.at[me], local_sem)
    own.start()
    own.wait()
    for copy in copies:
        copy.wait()


def exchange(x, ident):
    parts = x.shape[0]
    return pl.pallas_call(
        functools.partial(exchange_kernel, parts),
        out_shape=jax.ShapeDtypeStruct(x.shape, x.dtype),
        in_specs=[pl.BlockSpec(memory_space=pl.ANY)],
        out_specs=pl.BlockSpec(memory_space=pl.ANY),
        scratch_shapes=[
            pltpu.SemaphoreType.DMA,
            pltpu.SemaphoreType.DMA((parts - 1,)),
            pltpu.SemaphoreType.DMA((parts - 1,)),
        ],
        compiler_params=pltpu.CompilerParams(collective_id=ident, has_side_effects=True),
        cost_estimate=pl.CostEstimate(flops=0, bytes_accessed=50 * x.size, transcendentals=0),
    )(x)


def on_device(
    tokens,
    doc_lengths,
    cotangent,
    query_weight,
    key_weight,
    value_weight,
    out_weight,
    gate_weight,
    up_weight,
    down_weight,
    pre_attn_gain,
    post_attn_gain,
    pre_ffn_gain,
    post_ffn_gain,
    query_gain,
    key_gain,
):
    low = jnp.bfloat16
    full = jnp.float32
    dp = lax.axis_size("dp")
    mp = lax.axis_size("mp")
    shard = lax.axis_index("mp")
    rows, width = tokens.shape
    share = width // dp
    head_width = query_weight.shape[1]
    real_units = gate_weight.shape[1] // dp
    units = -(-real_units // 128) * 128
    spare = -(-(share + 1) // 16) * 16 - share
    own_rows = rows // mp
    own = (shard * own_rows, own_rows)

    gain_head = query_gain.shape[0]
    gains = jnp.concatenate(
        [pre_attn_gain, post_attn_gain, pre_ffn_gain, post_ffn_gain, query_gain, key_gain]
    )
    block = jnp.concatenate([query_weight, key_weight, value_weight, out_weight.T], axis=1)
    gains_row = jnp.pad(gains, (0, block.shape[1] - gains.shape[0]))[None]
    packed = jnp.concatenate([block, jnp.pad(gains_row, ((0, spare - 1), (0, 0)))], axis=0)
    packed = lax.all_gather(packed, "dp", axis=0, tiled=False)
    attn_w = packed[:, :share].reshape(width, 4 * head_width)
    qkv_w = attn_w[:, : 3 * head_width]
    out_wt = attn_w[:, 3 * head_width :]
    all_gains = packed[:, share].astype(full)
    gain_one, gain_two, gain_three, gain_four = (
        all_gains[:, i * share : (i + 1) * share].reshape(width) for i in range(4)
    )
    query_g = all_gains[:, 4 * share : 4 * share + gain_head].reshape(head_width)
    key_g = all_gains[:, 4 * share + gain_head : 4 * share + 2 * gain_head].reshape(head_width)

    ffn_block = jnp.stack([gate_weight, up_weight, down_weight.T], axis=0)
    ffn_block = ffn_block.reshape(3, share, dp, real_units).transpose(2, 1, 0, 3)
    ffn_block = jnp.pad(ffn_block, ((0, 0), (0, 0), (0, 0), (0, units - real_units)))
    ffn_w = exchange(ffn_block.reshape(dp, share, 3 * units), 3)
    ffn_w = ffn_w.reshape(width, 3 * units)
    glu_w = ffn_w[:, : 2 * units]
    down_wt = ffn_w[:, 2 * units :]

    inputs = tokens.astype(full)
    position, live_rows, allowed = layout(doc_lengths, rows // doc_lengths.shape[0])
    cosine, sine_table = angles(position, head_width)
    normed_in = normed(inputs, gain_one).astype(low)
    projected = matmul(normed_in, qkv_w)
    query_pre = projected[:, :head_width]
    key_pre = projected[:, head_width : 2 * head_width]
    value_low = projected[:, 2 * head_width :].astype(low)
    query_low = rotate(normed(query_pre, query_g), cosine, sine_table).astype(low)
    key_low = rotate(normed(key_pre, key_g), cosine, sine_table).astype(low)
    score_scale = head_width ** (-0.5)
    scores = inner_cols(query_low, key_low) * score_scale
    scores = jnp.where(allowed, scores, NEGATIVE)
    row_peak = jnp.max(scores, axis=1, keepdims=True)
    raised = jnp.exp(scores - row_peak)
    attention = raised / jnp.sum(raised, axis=1, keepdims=True)
    attention_low = attention.astype(low)
    attended = matmul(attention_low, value_low).astype(low)
    attn_part = inner_cols(attended, out_wt).astype(low)
    attn_sum = scatter(attn_part.reshape(mp, own_rows, width), ("mp",), 4)

    inputs_own = lax.dynamic_slice_in_dim(tokens, *own, axis=0).astype(full)
    upstream = lax.dynamic_slice_in_dim(cotangent, *own, axis=0).astype(full)
    live = lax.dynamic_slice_in_dim(live_rows, *own, axis=0)[:, None]

    def post_norm(values, factor):
        return normed(values, factor) * live

    attn_out, back_two = jax.vjp(post_norm, attn_sum, gain_two)
    middle = inputs_own + attn_out
    normed_mid_own, back_three = jax.vjp(normed, middle, gain_three)
    normed_mid = gather(normed_mid_own.astype(low), ("dp", "mp"), 1).reshape(-1, width)
    glu_pre = matmul(normed_mid, glu_w)
    gate_proj = glu_pre[:, :units]
    up_proj = glu_pre[:, units:]

    def glu(gate_in, up_in):
        return jax.nn.gelu(gate_in, approximate=True) * up_in

    hidden_full, back_glu = jax.vjp(glu, gate_proj, up_proj)
    hidden = hidden_full.astype(low)
    ffn_part = inner_cols(hidden, down_wt).astype(low)
    ffn_sum = scatter(ffn_part.reshape(dp * mp, own_rows, width), ("dp", "mp"), 2)
    ffn_out, back_four = jax.vjp(post_norm, ffn_sum, gain_four)
    mixed_own = (middle + ffn_out).astype(low)

    d_ffn_own, grad_four = back_four(upstream)
    d_ffn = gather(d_ffn_own.astype(low), ("dp", "mp"), 1).reshape(-1, width)
    grad_down_t = inner_rows(d_ffn, hidden)
    d_hidden = matmul(d_ffn, down_wt)
    d_gate, d_up = back_glu(d_hidden)
    d_glu = jnp.concatenate([d_gate.astype(low), d_up.astype(low)], axis=1)
    d_mid_part = inner_cols(d_glu, glu_w).astype(low)
    d_mid = scatter(d_mid_part.reshape(dp * mp, own_rows, width), ("dp", "mp"), 2)
    grad_glu = inner_rows(normed_mid, d_glu)
    ffn_grad = jnp.concatenate([grad_glu, grad_down_t], axis=1).astype(low)
    ffn_grad = ffn_grad.reshape(dp, share, 3 * units)
    ffn_grad = exchange(ffn_grad, 3)
    ffn_grad = ffn_grad.reshape(dp, share, 3, units)[..., :real_units].transpose(2, 1, 0, 3)
    ffn_grad = ffn_grad.reshape(3, share, dp * real_units).astype(full)

    d_mid_add, grad_three = back_three(d_mid)
    d_middle = upstream + d_mid_add
    d_attn_own, grad_two = back_two(d_middle)
    d_attn = gather(d_attn_own.astype(low), ("mp",), 5).reshape(rows, width)

    grad_out_t = inner_rows(d_attn, attended)
    d_attended = matmul(d_attn, out_wt).astype(low)
    d_value = inner_rows(attention_low, d_attended).astype(low)
    d_probs = inner_cols(d_attended, value_low)
    d_scores = attention * (d_probs - jnp.sum(attention * d_probs, axis=1, keepdims=True))
    d_scores = d_scores.astype(low)
    d_query_rot = matmul(d_scores, key_low) * score_scale
    d_key_rot = inner_rows(d_scores, query_low) * score_scale

    def turned(values, factor):
        return rotate(normed(values, factor), cosine, sine_table)

    _, back_query = jax.vjp(turned, query_pre, query_g)
    d_query_pre, grad_qgain = back_query(d_query_rot)
    _, back_key = jax.vjp(turned, key_pre, key_g)
    d_key_pre, grad_kgain = back_key(d_key_rot)
    d_qkv = jnp.concatenate([d_query_pre.astype(low), d_key_pre.astype(low), d_value], axis=1)
    d_in_part = inner_cols(d_qkv, qkv_w).astype(low)
    d_in = scatter(d_in_part.reshape(mp, own_rows, width), ("mp",), 4)
    grad_qkv = inner_rows(normed_in, d_qkv)
    _, back_one = jax.vjp(normed, inputs_own, gain_one)
    d_in_add, grad_one = back_one(d_in)
    tokens_grad_own = d_middle + d_in_add

    pieces = [g.reshape(dp, -1) for g in (grad_one, grad_two, grad_three, grad_four, grad_qgain, grad_kgain)]
    gains_grad = jnp.concatenate(pieces, axis=1)
    gains_grad = jnp.pad(gains_grad, ((0, 0), (0, 4 * head_width - gains_grad.shape[1])))
    weights_grad = jnp.concatenate([grad_qkv, grad_out_t], axis=1).reshape(dp, share, 4 * head_width)
    owned = jnp.concatenate(
        [weights_grad, jnp.pad(gains_grad[:, None], ((0, 0), (0, spare - 1), (0, 0)))], axis=1
    ).astype(low)
    owned = scatter(owned, ("dp",), 6)
    gains_back = jnp.pad(owned[share].reshape(2, 2 * head_width), ((0, spare), (0, 0)))[:spare]
    shared = jnp.concatenate(
        [owned[:share, head_width : 3 * head_width], gains_back], axis=0
    )
    shared = jnp.sum(gather(shared.astype(low), ("mp",), 7).astype(full), axis=0)
    kv_grad = shared[:share]
    gain_out = shared[share : share + 2].reshape(-1)
    mixed = lax.all_gather(mixed_own, "mp", axis=0, tiled=True)
    tokens_grad = lax.all_gather(tokens_grad_own.astype(low), "mp", axis=0, tiled=True).astype(full)
    return (
        mixed,
        tokens_grad,
        owned[:share, :head_width],
        kv_grad[:, :head_width],
        kv_grad[:, head_width:],
        owned[:share, 3 * head_width :].T,
        ffn_grad[0],
        ffn_grad[1],
        ffn_grad[2].T,
        gain_out[:share],
        gain_out[share : 2 * share],
        gain_out[2 * share : 3 * share],
        gain_out[3 * share : 4 * share],
        gain_out[4 * share : 4 * share + gain_head],
        gain_out[4 * share + gain_head : 4 * share + 2 * gain_head],
    )


def solution(mesh):
    placed = (
        P("dp", None),
        P("dp", None),
        P("dp", None),
        P("dp", "mp"),
        P("dp", None),
        P("dp", None),
        P("mp", "dp"),
        P("dp", "mp"),
        P("dp", "mp"),
        P("mp", "dp"),
        P("dp"),
        P("dp"),
        P("dp"),
        P("dp"),
        P("dp"),
        P("dp"),
    )
    return jax.shard_map(
        on_device,
        mesh=mesh,
        in_specs=placed,
        out_specs=(
            P("dp", None),
            P("dp", None),
            P("dp", "mp"),
            P("dp", None),
            P("dp", None),
            P("mp", "dp"),
            P("dp", "mp"),
            P("dp", "mp"),
            P("mp", "dp"),
            P("dp"),
            P("dp"),
            P("dp"),
            P("dp"),
            P("dp"),
            P("dp"),
        ),
        check_vma=False,
    )
```

```python
import functools
import math

import jax
import jax.numpy as jnp
from jax import lax
from jax.experimental import pallas as pl
from jax.experimental.pallas import tpu as pltpu
from jax.sharding import PartitionSpec as P

WINDOW = 512


EPSILON = 1e-06
THETA_BASE = 10000.0
NEGATIVE = -1e30


def matmul(left_op, right_op):
    return jnp.dot(left_op, right_op, preferred_element_type=jnp.float32)


def inner_rows(left_op, right_op):
    return lax.dot_general(
        left_op, right_op, (((0,), (0,)), ((), ())), preferred_element_type=jnp.float32
    )


def inner_cols(left_op, right_op):
    return lax.dot_general(
        left_op, right_op, (((1,), (1,)), ((), ())), preferred_element_type=jnp.float32
    )


def normed(values, factor):
    return values * lax.rsqrt(jnp.mean(values * values, axis=-1, keepdims=True) + EPSILON) * factor


def rotate(values, cosine, sine_table):
    half_width = values.shape[-1] // 2
    leading = values[..., :half_width]
    trailing = values[..., half_width:]
    return jnp.concatenate(
        [leading * cosine - trailing * sine_table, trailing * cosine + leading * sine_table],
        axis=-1,
    )


def layout(lengths, row_count):
    batches, docs = lengths.shape
    total = batches * row_count
    index = jnp.arange(total, dtype=jnp.int32)
    buffer = index // row_count
    inside = index % row_count
    order = jnp.arange(docs, dtype=jnp.int32)
    ends = jnp.sum(
        jnp.where(order[None, :, None] >= order[None, None, :], lengths[:, None, :], 0), axis=2
    )
    row_ends = jnp.repeat(ends, row_count, axis=0)
    row_lengths = jnp.repeat(lengths, row_count, axis=0)
    passed = inside[:, None] >= row_ends
    segment = jnp.sum(passed.astype(jnp.int32), axis=1)
    begins = jnp.sum(jnp.where(passed, row_lengths, 0), axis=1)
    position = inside - begins
    live_rows = (segment < docs).astype(jnp.float32)
    group = buffer * (docs + 1) + segment
    allowed = (
        (group[:, None] == group[None, :])
        & (index[None, :] <= index[:, None])
        & (index[:, None] - index[None, :] < WINDOW)
    )
    return (position, live_rows, allowed)


def angles(position, head_width):
    half_width = head_width // 2
    frequency = THETA_BASE ** (-2.0 * jnp.arange(half_width, dtype=jnp.float32) / head_width)
    turned = position.astype(jnp.float32)[:, None] * frequency[None, :]
    return (jnp.cos(turned), jnp.sin(turned))


MESH = pl.DeviceIdType.MESH


def axis_factors(axes):
    dims = []
    for axis in axes:
        left = lax.axis_size(axis)
        while left > 1:
            size = 4 if axis == "dp" and left >= 8 else 2
            left //= size
            dims.append((axis, size, left))
    return dims


def chunk_orders(dims, width):
    order = list(reversed(range(len(dims))))
    lanes = width // 128
    if dims[0][0] != "dp" or width % 128 or lanes < 2:
        return [(0, width, order)]
    swapped = list(order)
    at = 1 if len(dims) >= 3 else 0
    swapped[at], swapped[at + 1] = swapped[at + 1], swapped[at]
    half = (lanes + 1) // 2 * 128
    return [(0, half, order), (half, width - half, swapped)]


def places(dims):
    return [lax.rem(lax.axis_index(axis) // stride, size) for axis, size, stride in dims]


def peer(dims, coords, which, step):
    axis, size, stride = dims[which]
    target = lax.rem(coords[which] + step, size)
    device = {name: lax.axis_index(name) for name in ("dp", "mp")}
    device[axis] = device[axis] + (target - coords[which]) * stride
    return target, (device["dp"], device["mp"])


def greet(dims, coords, parts=0):
    barrier = pltpu.get_barrier_semaphore()
    count = 0
    for step in range(1, parts):
        device = (lax.rem(lax.axis_index("dp") + step, parts), lax.axis_index("mp"))
        pl.semaphore_signal(barrier, inc=1, device_id=device, device_id_type=MESH)
        count += 1
    for which, (axis, size, _) in enumerate(dims):
        if parts and axis == "dp":
            continue
        for step in range(1, size):
            _, device = peer(dims, coords, which, step)
            pl.semaphore_signal(barrier, inc=1, device_id=device, device_id_type=MESH)
            count += 1
    pl.semaphore_wait(barrier, count)


def slots_of(dims):
    firsts, total = [], 0
    for _, size, _ in dims:
        firsts.append(total)
        total += size - 1
    return firsts, total


def start_exchange(parts, x_ref, o_ref, local_sem, send_sem, recv_sem):
    me = lax.axis_index("dp")
    other = lax.axis_index("mp")
    copies = []
    for step in range(1, parts):
        target = lax.rem(me + step, parts)
        copy = pltpu.make_async_remote_copy(
            src_ref=x_ref.at[target],
            dst_ref=o_ref.at[me],
            send_sem=send_sem.at[step - 1],
            recv_sem=recv_sem.at[step - 1],
            device_id=(target, other),
            device_id_type=MESH,
        )
        copy.start()
        copies.append(copy)
    own = pltpu.make_async_copy(x_ref.at[me], o_ref.at[me], local_sem)
    own.start()
    copies.append(own)
    return copies


def exchange_scratch(parts):
    return [
        pltpu.SemaphoreType.DMA,
        pltpu.SemaphoreType.DMA((parts - 1,)),
        pltpu.SemaphoreType.DMA((parts - 1,)),
    ]


def gather_kernel(dims, chunks, firsts, parts, *refs):
    if parts:
        x_ref, ex_ref, o_ref, eo_ref, send_sem, recv_sem, *exchange_sems = refs
    else:
        x_ref, o_ref, send_sem, recv_sem = refs
    coords = places(dims)
    o_ref[tuple(coords)] = x_ref[...]
    greet(dims, coords, parts)

    def begin(k, stage):
        first, columns, order = chunks[k]
        order = order[::-1]
        done = order[:stage]
        which = order[stage]
        index = tuple(
            pl.ds(0, dims[i][1]) if i in done else coords[i] for i in range(len(dims))
        )
        block = o_ref.at[index + (slice(None), pl.ds(first, columns))]
        copies = []
        for step in range(1, dims[which][1]):
            slot = firsts[which] + step - 1
            _, device = peer(dims, coords, which, step)
            copy = pltpu.make_async_remote_copy(
                src_ref=block,
                dst_ref=block,
                send_sem=send_sem.at[k, slot],
                recv_sem=recv_sem.at[k, slot],
                device_id=device,
                device_id_type=MESH,
            )
            copy.start()
            copies.append(copy)
        return copies

    flying = [begin(k, 0) for k in range(len(chunks))]
    moving = start_exchange(parts, ex_ref, eo_ref, *exchange_sems) if parts else []
    for stage in range(len(dims)):
        for k in range(len(chunks)):
            for copy in flying[k]:
                copy.wait()
            if stage + 1 < len(dims):
                flying[k] = begin(k, stage + 1)
    for copy in moving:
        copy.wait()


def gather(x, axes, ident, extra=None):
    dims = axis_factors(axes)
    rows, width = x.shape
    chunks = chunk_orders(dims, width)
    firsts, slots = slots_of(dims)
    sizes = tuple(size for _, size, _ in dims)
    count = math.prod(sizes)
    nbytes = count * rows * width * x.dtype.itemsize
    more = [] if extra is None else [extra]
    parts = extra.shape[0] if more else 0
    anywhere = [pl.BlockSpec(memory_space=pl.ANY)] * len(more)
    out, *moved = pl.pallas_call(
        functools.partial(gather_kernel, dims, chunks, firsts, parts),
        out_shape=[jax.ShapeDtypeStruct(sizes + (rows, width), x.dtype)]
        + [jax.ShapeDtypeStruct(e.shape, e.dtype) for e in more],
        in_specs=[pl.BlockSpec(memory_space=pltpu.VMEM)] + anywhere,
        out_specs=[pl.BlockSpec(memory_space=pltpu.VMEM)] + anywhere,
        scratch_shapes=[
            pltpu.SemaphoreType.DMA((len(chunks), slots)),
            pltpu.SemaphoreType.DMA((len(chunks), slots)),
            *(exchange_scratch(parts) if more else []),
        ],
        compiler_params=pltpu.CompilerParams(
            collective_id=ident, has_side_effects=True, vmem_limit_bytes=nbytes + (8 << 20)
        ),
        cost_estimate=pl.CostEstimate(flops=0, bytes_accessed=20 * nbytes, transcendentals=0),
    )(x, *more)
    out = out.reshape(count, rows, width)
    return (out, moved[0]) if more else out


def scatter_kernel(dims, chunks, firsts, parts, *refs):
    if parts:
        x_ref, ex_ref, o_ref, eo_ref, acc, send_sem, recv_sem = refs[:7]
        exchange_sems, landed = refs[7:10], refs[10:]
    else:
        x_ref, o_ref, acc, send_sem, recv_sem, *landed = refs
    coords = places(dims)
    greet(dims, coords, parts)
    total = len(dims)

    def begin(k, stage):
        first, columns, order = chunks[k]
        done = order[:stage]
        which = order[stage]
        source = x_ref if stage == 0 else acc
        copies = []
        for step in range(1, dims[which][1]):
            slot = firsts[which] + step - 1
            target, device = peer(dims, coords, which, step)
            index = tuple(
                target if i == which else coords[i] if i in done else pl.ds(0, dims[i][1])
                for i in range(total)
            )
            copy = pltpu.make_async_remote_copy(
                src_ref=source.at[index + (slice(None), pl.ds(first, columns))],
                dst_ref=landed[k * total + stage].at[step - 1],
                send_sem=send_sem.at[k, slot],
                recv_sem=recv_sem.at[k, slot],
                device_id=device,
                device_id_type=MESH,
            )
            copy.start()
            copies.append(copy)
        return copies

    def add(k, stage):
        first, columns, order = chunks[k]
        which = order[stage]
        remain = [i for i in range(total) if i not in order[: stage + 1]]
        source = x_ref if stage == 0 else acc
        got = landed[k * total + stage]
        count = math.prod(dims[i][1] for i in remain)

        def one(n, carry):
            inner, left = {}, n
            for i in reversed(remain):
                inner[i] = lax.rem(left, dims[i][1])
                left = left // dims[i][1]
            index = tuple(inner[i] if i in inner else coords[i] for i in range(total))
            own = source[index + (slice(None), pl.ds(first, columns))].astype(jnp.float32)
            for step in range(1, dims[which][1]):
                place = (step - 1,) + tuple(inner[i] for i in remain)
                own = own + got[place].astype(jnp.float32)
            if remain:
                acc[index + (slice(None), pl.ds(first, columns))] = own.astype(acc.dtype)
            else:
                o_ref[:, pl.ds(first, columns)] = own
            return carry

        if count == 1:
            one(0, 0)
        else:
            lax.fori_loop(0, count, one, 0)

    flying = [begin(k, 0) for k in range(len(chunks))]
    moving = start_exchange(parts, ex_ref, eo_ref, *exchange_sems) if parts else []
    for stage in range(total):
        for k in range(len(chunks)):
            for copy in flying[k]:
                copy.wait()
            add(k, stage)
            if stage + 1 < total:
                flying[k] = begin(k, stage + 1)
    for copy in moving:
        copy.wait()


def scatter(x, axes, ident, extra=None):
    dims = axis_factors(axes)
    _, rows, width = x.shape
    chunks = chunk_orders(dims, width)
    firsts, slots = slots_of(dims)
    sizes = tuple(size for _, size, _ in dims)
    landed = []
    for _, columns, order in chunks:
        for stage, which in enumerate(order):
            remain = tuple(sizes[i] for i in range(len(dims)) if i not in order[: stage + 1])
            landed.append(
                pltpu.VMEM((sizes[which] - 1,) + remain + (rows, columns), x.dtype)
            )
    nbytes = math.prod(sizes) * rows * width * x.dtype.itemsize
    more = [] if extra is None else [extra]
    parts = extra.shape[0] if more else 0
    anywhere = [pl.BlockSpec(memory_space=pl.ANY)] * len(more)
    out, *moved = pl.pallas_call(
        functools.partial(scatter_kernel, dims, chunks, firsts, parts),
        out_shape=[jax.ShapeDtypeStruct((rows, width), jnp.float32)]
        + [jax.ShapeDtypeStruct(e.shape, e.dtype) for e in more],
        in_specs=[pl.BlockSpec(memory_space=pltpu.VMEM)] + anywhere,
        out_specs=[pl.BlockSpec(memory_space=pltpu.VMEM)] + anywhere,
        scratch_shapes=[
            pltpu.VMEM(sizes + (rows, width), x.dtype),
            pltpu.SemaphoreType.DMA((len(chunks), slots)),
            pltpu.SemaphoreType.DMA((len(chunks), slots)),
            *(exchange_scratch(parts) if more else []),
            *landed,
        ],
        compiler_params=pltpu.CompilerParams(
            collective_id=ident, has_side_effects=True, vmem_limit_bytes=3 * nbytes + (8 << 20)
        ),
        cost_estimate=pl.CostEstimate(flops=0, bytes_accessed=20 * nbytes, transcendentals=0),
    )(x.reshape(sizes + (rows, width)), *more)
    return (out, moved[0]) if more else out


def on_device(
    tokens,
    doc_lengths,
    cotangent,
    query_weight,
    key_weight,
    value_weight,
    out_weight,
    gate_weight,
    up_weight,
    down_weight,
    pre_attn_gain,
    post_attn_gain,
    pre_ffn_gain,
    post_ffn_gain,
    query_gain,
    key_gain,
):
    low = jnp.bfloat16
    full = jnp.float32
    dp = lax.axis_size("dp")
    mp = lax.axis_size("mp")
    shard = lax.axis_index("mp")
    rows, width = tokens.shape
    share = width // dp
    head_width = query_weight.shape[1]
    real_units = gate_weight.shape[1] // dp
    units = -(-real_units // 128) * 128
    spare = -(-(share + 1) // 16) * 16 - share
    own_rows = rows // mp
    own = (shard * own_rows, own_rows)

    gain_head = query_gain.shape[0]
    gains = jnp.concatenate(
        [pre_attn_gain, post_attn_gain, pre_ffn_gain, post_ffn_gain, query_gain, key_gain]
    )
    block = jnp.concatenate([query_weight, key_weight, value_weight, out_weight.T], axis=1)
    gains_row = jnp.pad(gains, (0, block.shape[1] - gains.shape[0]))[None]
    packed = jnp.concatenate([block, jnp.pad(gains_row, ((0, spare - 1), (0, 0)))], axis=0)
    packed = gather(packed, ("dp",), 10)
    attn_w = packed[:, :share].reshape(width, 4 * head_width)
    qkv_w = attn_w[:, : 3 * head_width]
    out_wt = attn_w[:, 3 * head_width :]
    all_gains = packed[:, share].astype(full)
    gain_one, gain_two, gain_three, gain_four = (
        all_gains[:, i * share : (i + 1) * share].reshape(width) for i in range(4)
    )
    query_g = all_gains[:, 4 * share : 4 * share + gain_head].reshape(head_width)
    key_g = all_gains[:, 4 * share + gain_head : 4 * share + 2 * gain_head].reshape(head_width)

    ffn_block = jnp.stack([gate_weight, up_weight, down_weight.T], axis=0)
    ffn_block = ffn_block.reshape(3, share, dp, real_units).transpose(2, 1, 0, 3)
    ffn_block = jnp.pad(ffn_block, ((0, 0), (0, 0), (0, 0), (0, units - real_units)))
    ffn_block = ffn_block.reshape(dp, share, 3 * units)

    inputs = tokens.astype(full)
    position, live_rows, allowed = layout(doc_lengths, rows // doc_lengths.shape[0])
    cosine, sine_table = angles(position, head_width)
    normed_in = normed(inputs, gain_one).astype(low)
    projected = matmul(normed_in, qkv_w)
    query_pre = projected[:, :head_width]
    key_pre = projected[:, head_width : 2 * head_width]
    value_low = projected[:, 2 * head_width :].astype(low)
    query_low = rotate(normed(query_pre, query_g), cosine, sine_table).astype(low)
    key_low = rotate(normed(key_pre, key_g), cosine, sine_table).astype(low)
    score_scale = head_width ** (-0.5)
    scores = inner_cols(query_low, key_low) * score_scale
    scores = jnp.where(allowed, scores, NEGATIVE)
    row_peak = jnp.max(scores, axis=1, keepdims=True)
    raised = jnp.exp(scores - row_peak)
    attention = raised / jnp.sum(raised, axis=1, keepdims=True)
    attention_low = attention.astype(low)
    attended = matmul(attention_low, value_low).astype(low)
    attn_part = inner_cols(attended, out_wt).astype(low)
    attn_sum = scatter(attn_part.reshape(mp, own_rows, width), ("mp",), 4)

    inputs_own = lax.dynamic_slice_in_dim(tokens, *own, axis=0).astype(full)
    upstream = lax.dynamic_slice_in_dim(cotangent, *own, axis=0).astype(full)
    live = lax.dynamic_slice_in_dim(live_rows, *own, axis=0)[:, None]

    def post_norm(values, factor):
        return normed(values, factor) * live

    attn_out, back_two = jax.vjp(post_norm, attn_sum, gain_two)
    middle = inputs_own + attn_out
    normed_mid_own, back_three = jax.vjp(normed, middle, gain_three)
    normed_mid, ffn_w = gather(normed_mid_own.astype(low), ("dp", "mp"), 8, ffn_block)
    normed_mid = normed_mid.reshape(-1, width)
    ffn_w = ffn_w.reshape(width, 3 * units)
    glu_w = ffn_w[:, : 2 * units]
    down_wt = ffn_w[:, 2 * units :]
    glu_pre = matmul(normed_mid, glu_w)
    gate_proj = glu_pre[:, :units]
    up_proj = glu_pre[:, units:]

    def glu(gate_in, up_in):
        return jax.nn.gelu(gate_in, approximate=True) * up_in

    hidden_full, back_glu = jax.vjp(glu, gate_proj, up_proj)
    hidden = hidden_full.astype(low)
    ffn_part = inner_cols(hidden, down_wt).astype(low)
    ffn_sum = scatter(ffn_part.reshape(dp * mp, own_rows, width), ("dp", "mp"), 2)
    ffn_out, back_four = jax.vjp(post_norm, ffn_sum, gain_four)
    mixed_own = (middle + ffn_out).astype(low)

    d_ffn_own, grad_four = back_four(upstream)
    d_ffn = gather(d_ffn_own.astype(low), ("dp", "mp"), 1).reshape(-1, width)
    grad_down_t = inner_rows(d_ffn, hidden)
    d_hidden = matmul(d_ffn, down_wt)
    d_gate, d_up = back_glu(d_hidden)
    d_glu = jnp.concatenate([d_gate.astype(low), d_up.astype(low)], axis=1)
    d_mid_part = inner_cols(d_glu, glu_w).astype(low)
    grad_glu = inner_rows(normed_mid, d_glu)
    ffn_grad = jnp.concatenate([grad_glu, grad_down_t], axis=1).astype(low)
    ffn_grad = ffn_grad.reshape(dp, share, 3 * units)
    d_mid, ffn_grad = scatter(
        d_mid_part.reshape(dp * mp, own_rows, width), ("dp", "mp"), 9, ffn_grad
    )
    ffn_grad = ffn_grad.reshape(dp, share, 3, units)[..., :real_units].transpose(2, 1, 0, 3)
    ffn_grad = ffn_grad.reshape(3, share, dp * real_units).astype(full)

    d_mid_add, grad_three = back_three(d_mid)
    d_middle = upstream + d_mid_add
    d_attn_own, grad_two = back_two(d_middle)
    d_attn = gather(d_attn_own.astype(low), ("mp",), 5).reshape(rows, width)

    grad_out_t = inner_rows(d_attn, attended)
    d_attended = matmul(d_attn, out_wt).astype(low)
    d_value = inner_rows(attention_low, d_attended).astype(low)
    d_probs = inner_cols(d_attended, value_low)
    d_scores = attention * (d_probs - jnp.sum(attention * d_probs, axis=1, keepdims=True))
    d_scores = d_scores.astype(low)
    d_query_rot = matmul(d_scores, key_low) * score_scale
    d_key_rot = inner_rows(d_scores, query_low) * score_scale

    def turned(values, factor):
        return rotate(normed(values, factor), cosine, sine_table)

    _, back_query = jax.vjp(turned, query_pre, query_g)
    d_query_pre, grad_qgain = back_query(d_query_rot)
    _, back_key = jax.vjp(turned, key_pre, key_g)
    d_key_pre, grad_kgain = back_key(d_key_rot)
    d_qkv = jnp.concatenate([d_query_pre.astype(low), d_key_pre.astype(low), d_value], axis=1)
    d_in_part = inner_cols(d_qkv, qkv_w).astype(low)
    d_in = scatter(d_in_part.reshape(mp, own_rows, width), ("mp",), 4)
    grad_qkv = inner_rows(normed_in, d_qkv)
    _, back_one = jax.vjp(normed, inputs_own, gain_one)
    d_in_add, grad_one = back_one(d_in)
    tokens_grad_own = d_middle + d_in_add

    pieces = [g.reshape(dp, -1) for g in (grad_one, grad_two, grad_three, grad_four, grad_qgain, grad_kgain)]
    gains_grad = jnp.concatenate(pieces, axis=1)
    gains_grad = jnp.pad(gains_grad, ((0, 0), (0, 4 * head_width - gains_grad.shape[1])))
    weights_grad = jnp.concatenate([grad_qkv, grad_out_t], axis=1).reshape(dp, share, 4 * head_width)
    owned = jnp.concatenate(
        [weights_grad, jnp.pad(gains_grad[:, None], ((0, 0), (0, spare - 1), (0, 0)))], axis=1
    ).astype(low)
    owned = scatter(owned, ("dp",), 6)
    gains_back = jnp.pad(owned[share].reshape(2, 2 * head_width), ((0, spare), (0, 0)))[:spare]
    shared = jnp.concatenate(
        [owned[:share, head_width : 3 * head_width], gains_back], axis=0
    )
    shared = jnp.sum(gather(shared.astype(low), ("mp",), 7).astype(full), axis=0)
    kv_grad = shared[:share]
    gain_out = shared[share : share + 2].reshape(-1)
    mixed = lax.all_gather(mixed_own, "mp", axis=0, tiled=True)
    tokens_grad = lax.all_gather(tokens_grad_own.astype(low), "mp", axis=0, tiled=True).astype(full)
    return (
        mixed,
        tokens_grad,
        owned[:share, :head_width],
        kv_grad[:, :head_width],
        kv_grad[:, head_width:],
        owned[:share, 3 * head_width :].T,
        ffn_grad[0],
        ffn_grad[1],
        ffn_grad[2].T,
        gain_out[:share],
        gain_out[share : 2 * share],
        gain_out[2 * share : 3 * share],
        gain_out[3 * share : 4 * share],
        gain_out[4 * share : 4 * share + gain_head],
        gain_out[4 * share + gain_head : 4 * share + 2 * gain_head],
    )


def solution(mesh):
    placed = (
        P("dp", None),
        P("dp", None),
        P("dp", None),
        P("dp", "mp"),
        P("dp", None),
        P("dp", None),
        P("mp", "dp"),
        P("dp", "mp"),
        P("dp", "mp"),
        P("mp", "dp"),
        P("dp"),
        P("dp"),
        P("dp"),
        P("dp"),
        P("dp"),
        P("dp"),
    )
    return jax.shard_map(
        on_device,
        mesh=mesh,
        in_specs=placed,
        out_specs=(
            P("dp", None),
            P("dp", None),
            P("dp", "mp"),
            P("dp", None),
            P("dp", None),
            P("mp", "dp"),
            P("dp", "mp"),
            P("dp", "mp"),
            P("mp", "dp"),
            P("dp"),
            P("dp"),
            P("dp"),
            P("dp"),
            P("dp"),
            P("dp"),
        ),
        check_vma=False,
    )
```
